512 devices in a mesh: pb: 8 (over y), ka: 16 (over z, core), ha: 4 (over x).
Axes of the slice: x: 4, y: 8, z: 8, core: 2. Of those that a mesh axis runs over, the one named last changes fastest.
Arguments:
- latent: bfloat16 [2048, 1536], P('pb'), may hold values from -6 to 6
- query_weight: bfloat16 [1536, 8192], P(None, ('ka', 'ha')), may hold values from -0.15625 to 0.15625
- head_weights: bfloat16 [2048, 64], P('pb', ('ka', 'ha')), may hold values from -0.75 to 0.75
- raw_keys: bfloat16 [65536, 128], P(('ka', 'ha')), may hold values from -6 to 6
- key_gain: float32 [128], replicated, may hold values from 0.1 to 1.9
- key_bias: float32 [128], replicated, may hold values from -3 to 3
- query_start: int32 [8], P('pb'), may hold values from 0 to 65280, as said below
- key_order: int32 [16], P('ka'), may hold values from 0 to 15, each once
Outputs:
- index_scores: float32 [2048, 65536], P('pb', ('ka', 'ha'))
The draws below stay inside these ranges and needn't reach their ends.
Inputs may be any that keep to these rules, and one draw needn't show every extreme that they name: `query_start`: entries are distinct multiples of 256; the last block (position 65280) is always among them. `key_order`: each block number 0 to 15 appears exactly once.
All inputs are finite; a program needn't handle non-finite values.
Results may differ from the reference program's by a relative error of at most 0.007.
Values may be sent and summed in bfloat16 or wider, within the bound.
No kernel may reach another device: no remote copies, remote signals or barrier semaphores. Data moves between devices by JAX's collectives and lax.ppermute only.
A program may use at most 128 MiB of HBM per device.

```python
import jax
import jax.numpy as jnp
from jax import lax

DLAT = 1536
HEADS = 64
HDIM = 128
QB = 256
KB = 4096
QTOK = 2048
SEQ = 65536
N_PB = 8
N_KA = 16


def draw_query_start(key, part):
    key = jax.random.fold_in(key, 7)
    first_key, second_key = jax.random.split(key)
    block_total = SEQ // QB
    others = jax.random.permutation(first_key, block_total - 1)[:N_PB - 1].astype(jnp.int32)
    chosen = jnp.concatenate([jnp.array([block_total - 1], jnp.int32), others])
    shuffle = jax.random.permutation(second_key, N_PB)
    return (chosen[shuffle] * QB).astype(jnp.int32)


def level_of(stream_key, extent, pieces, low, largest):
    def one(axis_at, shards_of):
        steps = jax.random.uniform(jax.random.fold_in(jax.random.fold_in(stream_key, 6), axis_at), (shards_of,), jnp.float32, low / len(pieces), largest / len(pieces))
        return jnp.repeat(jnp.exp(steps), extent[axis_at] // shards_of).reshape((-1,) + (1,) * (len(extent) - axis_at - 1))

    loudness = one(*pieces[0])
    for cut in pieces[1:]:
        loudness = loudness * one(*cut)
    return loudness


def normal_values(rng, extent, deviation, most, pieces=(), kind=jnp.bfloat16):
    gain = level_of(rng, extent, pieces, -0.22, 0.18) if pieces else 1.0
    entries = jax.random.normal(rng, extent, jnp.float32) * deviation * gain
    return jnp.minimum(jnp.maximum(entries, -most), most).astype(kind)


def setup_inputs(seed: int = 0) -> dict:
    streams_of = jax.random.split(jax.random.key(seed), 9)
    return {
        "latent": normal_values(streams_of[0], (QTOK, DLAT), 1.0, 6.0, ((0, 8),)),
        "query_weight": normal_values(streams_of[1], (DLAT, HEADS * HDIM), DLAT ** -0.5, 0.15625, ((1, 64),)),
        "head_weights": normal_values(streams_of[2], (QTOK, HEADS), 0.125, 0.75, ((0, 8), (1, 64))),
        "raw_keys": normal_values(streams_of[3], (SEQ, HDIM), 1.0, 6.0, ((0, 64),)),
        "key_gain": jnp.clip(1.0 + 0.18 * jax.random.normal(streams_of[4], (HDIM,), jnp.float32), 0.1, 1.9),
        "key_bias": normal_values(streams_of[5], (HDIM,), 0.5, 3.0, (), jnp.float32),
        "query_start": draw_query_start(jax.random.fold_in(streams_of[8], 71), 0),
        "key_order": jax.random.permutation(streams_of[7], N_KA).astype(jnp.int32),
    }


def normalize_keys(raw_keys, key_gain, key_bias):
    values = raw_keys.astype(jnp.float32)
    center = lax.optimization_barrier(jnp.mean(values, axis=-1, keepdims=True))
    spread = lax.optimization_barrier(jnp.mean(jnp.square(values - center), axis=-1, keepdims=True))
    scaled = (values - center) * lax.rsqrt(spread + 1e-06)
    return (scaled * key_gain + key_bias).astype(jnp.bfloat16)

def reference(latent, query_weight, head_weights, raw_keys, key_gain, key_bias, query_start, key_order):
    queries = jnp.dot(latent, query_weight, preferred_element_type=jnp.float32).astype(jnp.bfloat16)
    flat_queries = queries.astype(jnp.float32).reshape(QTOK * HEADS, HDIM)
    weights_full = head_weights.astype(jnp.float32)
    normed = normalize_keys(raw_keys, key_gain, key_bias).astype(jnp.float32)
    query_pos = (query_start.astype(jnp.int32)[:, None] + jnp.arange(QB, dtype=jnp.int32)[None, :]).reshape(QTOK)
    key_pos = (key_order.astype(jnp.int32)[:, None] * KB + jnp.arange(KB, dtype=jnp.int32)[None, :]).reshape(SEQ)
    block_width = min(512, SEQ)
    blocks = SEQ // block_width

    def one_block(block_pair):
        block_keys, block_pos = block_pair
        scores = jnp.dot(flat_queries, block_keys.T, precision=lax.Precision.HIGHEST)
        scores = scores.reshape(QTOK, HEADS, block_width)
        active = jax.nn.relu(scores) * HDIM ** (-0.5)
        totals = jnp.einsum('qhk,qh->qk', active, weights_full, precision=lax.Precision.HIGHEST)
        return jnp.where(block_pos[None, :] <= query_pos[:, None], totals, jnp.zeros_like(totals))
    tiles = lax.map(one_block, (normed.reshape(blocks, block_width, HDIM), key_pos.reshape(blocks, block_width)))
    return tiles.transpose(1, 0, 2).reshape(QTOK, SEQ)
```

```python
import functools

import jax
import jax.numpy as jnp
from jax import lax
from jax.experimental import pallas as pl
from jax.experimental.pallas import tpu as pltpu
from jax.sharding import PartitionSpec as P

VMEM = pltpu.VMEM
SMEM = pltpu.SMEM
TOKENS = 256
KEYS = 1024
HDIM = 128
ROWS = TOKENS + 16
TB = 32
AHEAD = 6
FLAT = ("ka", "ha")


def front_kernel(latent_ref, weight_ref, head_ref, raw_ref, gain_ref, bias_ref, block_ref, keys_ref):
    queries = jnp.dot(
        latent_ref[...], weight_ref[...], preferred_element_type=jnp.float32
    ).astype(jnp.bfloat16)
    row = head_ref[...].astype(jnp.float32)
    row_at = lax.broadcasted_iota(jnp.int32, (16, HDIM), 0)
    first = jnp.broadcast_to(row[:, :HDIM], (16, HDIM))
    second = jnp.broadcast_to(row[:, HDIM:], (16, HDIM))
    tail = jnp.where(row_at == 0, first, jnp.where(row_at == 1, second, 0.0)).astype(jnp.bfloat16)
    for i in range(block_ref.shape[0]):
        block_ref[i, :TOKENS, :] = queries
        block_ref[i, TOKENS:, :] = tail
    values = raw_ref[...].astype(jnp.float32)
    center = jnp.mean(values, axis=-1, keepdims=True)
    moved = values - center
    spread = jnp.mean(jnp.square(moved), axis=-1, keepdims=True)
    scaled = moved * lax.rsqrt(spread + 1e-06)
    keys_ref[...] = (scaled * gain_ref[...] + bias_ref[...]).astype(jnp.bfloat16)


def front(latent, query_weight, head_row, raw_keys, gain, bias, copies):
    return pl.pallas_call(
        front_kernel,
        out_shape=(
            jax.ShapeDtypeStruct((copies, ROWS, HDIM), jnp.bfloat16),
            jax.ShapeDtypeStruct((KEYS, HDIM), jnp.bfloat16),
        ),
        in_specs=[pl.BlockSpec(memory_space=VMEM)] * 6,
        out_specs=[pl.BlockSpec(memory_space=VMEM)] * 2,
        compiler_params=pltpu.CompilerParams(vmem_limit_bytes=24 * 2**20),
        cost_estimate=pl.CostEstimate(flops=2 * 256 * 1536 * 128, bytes_accessed=2 * 2**20, transcendentals=1024),
        name="front",
    )(latent, query_weight, head_row, raw_keys, gain, bias)


def score_kernel(*refs, chunks, has_total):
    parts = refs[:chunks]
    keys_ref = refs[chunks]
    total_ref = refs[chunks + 1] if has_total else None
    out_ref = refs[-1]
    heads = [(p, h) for p in parts for h in range(p.shape[0])]
    steps = [(t, i) for t in range(TOKENS // TB) for i in range(len(heads))]
    slots = AHEAD + 1

    def scoped(*accs):
        def acc(m, s, j):
            return accs[(m * slots + s) * 2 + j]

        for m in range(2):
            a = keys_ref[512 * m : 512 * m + 256, :]
            b = keys_ref[512 * m + 256 : 512 * m + 512, :]
            pltpu.matmul_push_rhs(jnp.concatenate([a, b], axis=1), 0, m, transpose=True)
        zero = jnp.zeros((TB, HDIM), jnp.bfloat16)
        columns = [p[h, TOKENS:, :].astype(jnp.float32).T for p, h in heads]

        def issue(n):
            t, i = steps[n]
            p, h = heads[i]
            q = p[h, t * TB : (t + 1) * TB, :]
            low = jnp.concatenate([q, zero], axis=1)
            high = jnp.concatenate([zero, q], axis=1)
            for m in range(2):
                pltpu.matmul_acc_lhs(acc(m, n % slots, 0), low, load_staged_rhs=0 if n == 0 else None)
                pltpu.matmul_acc_lhs(acc(m, n % slots, 1), high)

        for n in range(min(AHEAD, len(steps))):
            issue(n)
        sums = None
        per_row = HDIM // TB
        for n, (t, i) in enumerate(steps):
            if n + AHEAD < len(steps):
                issue(n + AHEAD)
            if i == 0:
                if total_ref is None:
                    sums = [jnp.zeros((TB, 256), jnp.float32) for _ in range(4)]
                else:
                    sums = [total_ref[t * TB : (t + 1) * TB, 256 * g : 256 * (g + 1)] for g in range(4)]
            at = (t % per_row) * TB
            weight = columns[i][at : at + TB, t // per_row : t // per_row + 1]
            weight = jnp.broadcast_to(weight, (TB, 256))
            for m in range(2):
                for j in range(2):
                    score = pltpu.matmul_pop(acc(m, n % slots, j))
                    sums[2 * m + j] = sums[2 * m + j] + jnp.maximum(score, 0.0) * weight
            if i == len(heads) - 1:
                for g in range(4):
                    out_ref[t * TB : (t + 1) * TB, 256 * g : 256 * (g + 1)] = sums[g].astype(out_ref.dtype)

    pl.run_scoped(scoped, *[pltpu.ACC(m)((TB, 256), jnp.float32) for m in range(2) for _ in range(2 * slots)])


def scores(parts, keys, total=None, out_dtype=jnp.float32, name="scores"):
    heads = sum(p.shape[0] for p in parts)
    extra = [] if total is None else [total]
    return pl.pallas_call(
        functools.partial(score_kernel, chunks=len(parts), has_total=total is not None),
        out_shape=jax.ShapeDtypeStruct((TOKENS, KEYS), out_dtype),
        in_specs=[pl.BlockSpec(memory_space=VMEM)] * (len(parts) + 1 + len(extra)),
        out_specs=pl.BlockSpec(memory_space=VMEM),
        compiler_params=pltpu.CompilerParams(vmem_limit_bytes=24 * 2**20),
        cost_estimate=pl.CostEstimate(
            flops=4 * heads * TOKENS * KEYS * HDIM, bytes_accessed=2**21, transcendentals=0
        ),
        name=name,
    )(*parts, keys, *extra)


def finish_kernel(place_ref, own_ref, other_ref, out_ref):
    scale = HDIM ** (-0.5)
    rows = out_ref.shape[0]
    query = place_ref[0] + lax.broadcasted_iota(jnp.int32, (rows, 256), 0)
    for g in range(KEYS // 256):
        key = place_ref[1] + 256 * g + lax.broadcasted_iota(jnp.int32, (rows, 256), 1)
        at = slice(256 * g, 256 * (g + 1))
        total = (own_ref[:, at] + other_ref[:, at].astype(jnp.float32)) * scale
        out_ref[:, at] = jnp.where(key <= query, total, 0.0)


def finish(place, own, other):
    return pl.pallas_call(
        finish_kernel,
        out_shape=jax.ShapeDtypeStruct((TOKENS, KEYS), jnp.float32),
        in_specs=[pl.BlockSpec(memory_space=SMEM)] + [pl.BlockSpec(memory_space=VMEM)] * 2,
        out_specs=pl.BlockSpec(memory_space=VMEM),
        compiler_params=pltpu.CompilerParams(vmem_limit_bytes=24 * 2**20),
        cost_estimate=pl.CostEstimate(flops=2**20, bytes_accessed=3 * 2**20, transcendentals=0),
        name="finish",
    )(place, own, other)


def layout(z_size, x_size):
    def flat(z, core, x):
        return ((z % z_size) * 2 + core) * x_size + x % x_size

    sites = [(z, x) for z in range(z_size) for x in range(x_size)]
    groups = [
        [flat(z, core, x) for z, x in sites if (z - x) % x_size == coset]
        for core in range(2)
        for coset in range(x_size)
    ]

    def moved(dz, dx):
        return [
            (flat(z, core, x), flat(z + sign * dz, core, x + sign * dx))
            for core, sign in ((0, 1), (1, -1))
            for z, x in sites
        ]

    swap = [(flat(z, core, x), flat(z, 1 - core, x)) for z, x in sites for core in range(2)]
    return groups, moved, swap


def per_device(
    latent, query_weight, head_weights, raw_keys, key_gain, key_bias, query_start, key_order
):
    ka, ha = lax.axis_size("ka"), lax.axis_size("ha")
    groups, moved, swap = layout(ka // 2, ha)
    block, keys = front(
        latent,
        query_weight,
        head_weights.reshape(1, TOKENS),
        raw_keys,
        key_gain.reshape(1, HDIM),
        key_bias.reshape(1, HDIM),
        len(groups[0]),
    )
    here = lax.all_to_all(block, FLAT, 0, 0, axis_index_groups=groups)
    other_keys = lax.ppermute(keys, FLAT, swap)
    along_z = lax.ppermute(here, FLAT, moved(1, 0))
    along_x = lax.ppermute(here, FLAT, moved(0, 1))
    diagonal = lax.ppermute(here, FLAT, moved(1, -1))

    own = scores([here], keys, name="own0")
    other = scores([here], other_keys, name="other0")
    other = scores([along_z], other_keys, other, name="other1")
    own = scores([along_z], keys, own, name="own1")
    other = scores([along_x], other_keys, other, name="other2")
    own = scores([along_x], keys, own, name="own2")
    other = scores([diagonal], other_keys, other, jnp.bfloat16, name="other3")
    received = lax.ppermute(other, FLAT, swap)
    own = scores([diagonal], keys, own, name="own3")
    key_begin = (key_order[0] * ha + lax.axis_index("ha")) * KEYS
    place = jnp.stack([query_start[0], key_begin]).astype(jnp.int32)
    return finish(place, own, received)


def solution(mesh):
    in_specs = (
        P("pb", None),
        P(None, ("ka", "ha")),
        P("pb", ("ka", "ha")),
        P(("ka", "ha"), None),
        P(),
        P(),
        P("pb"),
        P("ka"),
    )
    out_specs = P("pb", ("ka", "ha"))
    return jax.shard_map(
        per_device, mesh=mesh, in_specs=in_specs, out_specs=out_specs, check_vma=False
    )
```

```python
import functools

import jax
import jax.numpy as jnp
from jax import lax
from jax.experimental import pallas as pl
from jax.experimental.pallas import tpu as pltpu
from jax.sharding import PartitionSpec as P

VMEM = pltpu.VMEM
HBM = pltpu.HBM
TOKENS = 256
KEYS = 1024
HDIM = 128
ROWS = TOKENS + 16
TB = 32
AHEAD = 6
FLAT = ("ka", "ha")


def front_kernel(
    latent_hbm, weight_hbm, head_hbm, raw_hbm, gain_hbm, bias_hbm,
    block_hbm, keys_hbm,
    latent_ref, weight_ref, head_ref, raw_ref, gain_ref, bias_ref,
    block_ref, keys_ref, sems,
):
    sources = (latent_hbm, weight_hbm, head_hbm, raw_hbm, gain_hbm, bias_hbm)
    targets = (latent_ref, weight_ref, head_ref, raw_ref, gain_ref, bias_ref)
    copies = [
        pltpu.make_async_copy(source, target, sems.at[i])
        for i, (source, target) in enumerate(zip(sources, targets))
    ]
    for copy in copies:
        copy.start()
    for copy in copies[:3]:
        copy.wait()
    block_ref[:TOKENS, :] = jnp.dot(
        latent_ref[...], weight_ref[...], preferred_element_type=jnp.float32
    ).astype(jnp.bfloat16)
    row = head_ref[...].astype(jnp.float32)
    tail_rows = ROWS - TOKENS
    row_at = lax.broadcasted_iota(jnp.int32, (tail_rows, HDIM), 0)
    first = jnp.broadcast_to(row[:, :HDIM], (tail_rows, HDIM))
    second = jnp.broadcast_to(row[:, HDIM:], (tail_rows, HDIM))
    block_ref[TOKENS:, :] = jnp.where(
        row_at == 0, first, jnp.where(row_at == 1, second, 0.0)
    ).astype(jnp.bfloat16)
    outs = []
    for i in range(block_hbm.shape[0]):
        outs.append(pltpu.make_async_copy(block_ref, block_hbm.at[i], sems.at[6 + i]))
        outs[-1].start()
    for copy in copies[3:]:
        copy.wait()
    values = raw_ref[...].astype(jnp.float32)
    center = jnp.mean(values, axis=-1, keepdims=True)
    moved = values - center
    spread = jnp.mean(jnp.square(moved), axis=-1, keepdims=True)
    scaled = moved * lax.rsqrt(spread + 1e-06)
    keys_ref[...] = (scaled * gain_ref[...] + bias_ref[...]).astype(jnp.bfloat16)
    outs.append(pltpu.make_async_copy(keys_ref, keys_hbm, sems.at[0]))
    outs[-1].start()
    for copy in outs:
        copy.wait()


def front(arrays, copies):
    outs = (
        jax.ShapeDtypeStruct((copies, ROWS, HDIM), jnp.bfloat16),
        jax.ShapeDtypeStruct((KEYS, HDIM), jnp.bfloat16),
    )
    return pl.pallas_call(
        front_kernel,
        out_shape=outs,
        in_specs=[pl.BlockSpec(memory_space=HBM)] * len(arrays),
        out_specs=[pl.BlockSpec(memory_space=HBM)] * len(outs),
        scratch_shapes=[VMEM(a.shape, a.dtype) for a in arrays]
        + [VMEM(outs[0].shape[1:], jnp.bfloat16), VMEM(outs[1].shape, jnp.bfloat16)]
        + [pltpu.SemaphoreType.DMA((6 + copies,))],
        compiler_params=pltpu.CompilerParams(vmem_limit_bytes=60 * 2**20),
        cost_estimate=pl.CostEstimate(flops=2 * 256 * 1536 * 128, bytes_accessed=2 * 2**20, transcendentals=1024),
        name="front",
    )(*arrays)


def score_steps(part_refs, keys_refs, total_refs, flush):
    heads = [(p, h) for p in part_refs for h in range(p.shape[0])]
    blocks = TOKENS // TB
    steps = [(k, t, i) for k in range(len(keys_refs)) for t in range(blocks) for i in range(len(heads))]
    slots = AHEAD + 1

    def scoped(*accs):
        def acc(m, s, j):
            return accs[(m * slots + s) * 2 + j]

        zero = jnp.zeros((TB, HDIM), jnp.bfloat16)
        columns = [p[h, TOKENS:, :].astype(jnp.float32).T for p, h in heads]
        for k, keys_ref in enumerate(keys_refs):
            for m in range(2):
                a = keys_ref[512 * m : 512 * m + 256, :]
                b = keys_ref[512 * m + 256 : 512 * m + 512, :]
                pltpu.matmul_push_rhs(jnp.concatenate([a, b], axis=1), k, m, transpose=True)

        def issue(n):
            k, t, i = steps[n]
            p, h = heads[i]
            q = p[h, t * TB : (t + 1) * TB, :]
            low = jnp.concatenate([q, zero], axis=1)
            high = jnp.concatenate([zero, q], axis=1)
            staged = k if t == 0 and i == 0 else None
            for m in range(2):
                pltpu.matmul_acc_lhs(acc(m, n % slots, 0), low, load_staged_rhs=staged)
                pltpu.matmul_acc_lhs(acc(m, n % slots, 1), high)

        for n in range(AHEAD):
            issue(n)
        sums = None
        per_row = HDIM // TB
        for n, (k, t, i) in enumerate(steps):
            if n + AHEAD < len(steps):
                issue(n + AHEAD)
            rows = slice(t * TB, (t + 1) * TB)
            if i == 0:
                if not total_refs:
                    sums = [jnp.zeros((TB, 256), jnp.float32) for _ in range(4)]
                else:
                    sums = [total_refs[k][rows, 256 * g : 256 * (g + 1)] for g in range(4)]
            at = (t % per_row) * TB
            weight = columns[i][at : at + TB, t // per_row : t // per_row + 1]
            weight = jnp.broadcast_to(weight, (TB, 256))
            for m in range(2):
                for j in range(2):
                    score = pltpu.matmul_pop(acc(m, n % slots, j))
                    sums[2 * m + j] = sums[2 * m + j] + jnp.maximum(score, 0.0) * weight
            if i == len(heads) - 1:
                flush(k, t, sums)

    pl.run_scoped(scoped, *[pltpu.ACC(m)((TB, 256), jnp.float32) for m in range(2) for _ in range(2 * slots)])


def score_kernel(*refs, parts, sets, has_totals, has_place):
    if has_place:
        start_ref, order_ref, *refs, reach_ref = refs
        key_begin = (order_ref[...] * lax.axis_size("ha") + lax.axis_index("ha")) * KEYS
        reach_ref[...] = jnp.broadcast_to(start_ref[...] - key_begin, reach_ref.shape)
    part_refs, refs = refs[:parts], refs[parts:]
    keys_refs, refs = refs[:sets], refs[sets:]
    total_refs, out_refs = (refs[:sets], refs[sets:]) if has_totals else ((), refs)

    def flush(k, t, sums):
        rows = slice(t * TB, (t + 1) * TB)
        for g in range(4):
            out_refs[k][rows, 256 * g : 256 * (g + 1)] = sums[g].astype(out_refs[k].dtype)

    score_steps(part_refs, keys_refs, total_refs, flush)


def score_cost(parts, sets):
    heads = sum(p.shape[0] for p in parts)
    return pl.CostEstimate(
        flops=heads * sets * 2**14, bytes_accessed=2**14, transcendentals=0
    )


def scores(parts, keys, totals=(), place=(), out_dtype=jnp.float32, name="scores"):
    operands = (*place, *parts, *keys, *totals)
    outs = [jax.ShapeDtypeStruct((TOKENS, KEYS), out_dtype) for _ in keys]
    if place:
        outs.append(jax.ShapeDtypeStruct((TB, 256), jnp.int32))
    return pl.pallas_call(
        functools.partial(
            score_kernel, parts=len(parts), sets=len(keys), has_totals=bool(totals), has_place=bool(place)
        ),
        out_shape=outs,
        in_specs=[pl.BlockSpec(memory_space=VMEM)] * len(operands),
        out_specs=[pl.BlockSpec(memory_space=VMEM)] * len(outs),
        compiler_params=pltpu.CompilerParams(vmem_limit_bytes=24 * 2**20),
        cost_estimate=score_cost(parts, len(keys)),
        name=name,
    )(*operands)


def finish_kernel(part_ref, keys_ref, total_ref, reach_ref, other_ref, out_hbm, out_ref, sems):
    scale = HDIM ** (-0.5)
    reach = reach_ref[...]
    ahead = lax.broadcasted_iota(jnp.int32, (TB, 256), 1) - lax.broadcasted_iota(jnp.int32, (TB, 256), 0)
    copies = []

    def flush(k, t, sums):
        rows = slice(t * TB, (t + 1) * TB)
        for g in range(4):
            at = slice(256 * g, 256 * (g + 1))
            total = (sums[g] + other_ref[rows, at].astype(jnp.float32)) * scale
            out_ref[rows, at] = jnp.where(ahead <= reach + (t * TB - 256 * g), total, 0.0)
        copies.append(pltpu.make_async_copy(out_ref.at[rows], out_hbm.at[rows], sems.at[t]))
        copies[-1].start()
        if t == TOKENS // TB - 1:
            for copy in copies:
                copy.wait()

    score_steps((part_ref,), (keys_ref,), (total_ref,), flush)


def finish(part, keys, total, reach, other):
    return pl.pallas_call(
        finish_kernel,
        out_shape=jax.ShapeDtypeStruct((TOKENS, KEYS), jnp.float32),
        in_specs=[pl.BlockSpec(memory_space=VMEM)] * 5,
        out_specs=pl.BlockSpec(memory_space=HBM),
        scratch_shapes=[VMEM((TOKENS, KEYS), jnp.float32), pltpu.SemaphoreType.DMA((TOKENS // TB,))],
        compiler_params=pltpu.CompilerParams(vmem_limit_bytes=24 * 2**20),
        cost_estimate=score_cost((part,), 1),
        name="finish",
    )(part, keys, total, reach, other)


def layout(z_size, x_size):
    def flat(z, core, x):
        return ((z % z_size) * 2 + core) * x_size + x % x_size

    sites = [(z, x) for z in range(z_size) for x in range(x_size)]
    groups = [
        [flat(z, core, x) for z, x in sites if (z - x) % x_size == coset]
        for core in range(2)
        for coset in range(x_size)
    ]

    def moved(dz, dx):
        return [
            (flat(z, core, x), flat(z + sign * dz, core, x + sign * dx))
            for core, sign in ((0, 1), (1, -1))
            for z, x in sites
        ]

    swap = [(flat(z, core, x), flat(z, 1 - core, x)) for z, x in sites for core in range(2)]
    return groups, moved, swap


def per_device(
    latent, query_weight, head_weights, raw_keys, key_gain, key_bias, query_start, key_order
):
    ka, ha = lax.axis_size("ka"), lax.axis_size("ha")
    groups, moved, swap = layout(ka // 2, ha)
    block, keys = front(
        (
            latent,
            query_weight,
            head_weights.reshape(1, TOKENS),
            raw_keys,
            key_gain.reshape(1, HDIM),
            key_bias.reshape(1, HDIM),
        ),
        len(groups[0]),
    )
    here = lax.all_to_all(block, FLAT, 0, 0, axis_index_groups=groups)
    diagonal = lax.ppermute(here, FLAT, moved(1, -1))
    along_z = lax.ppermute(here, FLAT, moved(1, 0))
    along_x = lax.ppermute(here, FLAT, moved(0, 1))

    (own,) = scores((here,), (keys,), name="here_own")
    own, swapped = lax.optimization_barrier((own, keys))
    other_keys = lax.ppermute(swapped, FLAT, swap)
    place = (query_start.reshape(1, 1), key_order.reshape(1, 1))
    own, reach = scores((diagonal,), (keys,), (own,), place, name="diagonal_own")
    own, other_keys = lax.optimization_barrier((own, other_keys))
    (other,) = scores((here, diagonal), (other_keys,), name="here_diagonal_other")
    (other,) = scores((along_z,), (other_keys,), (other,), name="z_other")
    (other,) = scores((along_x,), (other_keys,), (other,), out_dtype=jnp.bfloat16, name="x_other")
    received = lax.ppermute(other, FLAT, swap)
    own, other = lax.optimization_barrier((own, other))
    (own,) = scores((along_z,), (keys,), (own,), name="z_own")
    return finish(along_x, keys, own, reach, received)


def solution(mesh):
    in_specs = (
        P("pb", None),
        P(None, ("ka", "ha")),
        P("pb", ("ka", "ha")),
        P(("ka", "ha"), None),
        P(),
        P(),
        P("pb"),
        P("ka"),
    )
    out_specs = P("pb", ("ka", "ha"))
    return jax.shard_map(
        per_device, mesh=mesh, in_specs=in_specs, out_specs=out_specs, check_vma=False
    )
```

```python
import functools

import jax
import jax.numpy as jnp
from jax import lax
from jax.experimental import pallas as pl
from jax.experimental.pallas import tpu as pltpu
from jax.sharding import PartitionSpec as P

VMEM = pltpu.VMEM
HBM = pltpu.HBM
TOKENS = 256
KEYS = 1024
HDIM = 128
ROWS = TOKENS + 16
TB = 32
AHEAD = 6
EARLY = 2
FLAT = ("ka", "ha")


def front_kernel(
    raw_hbm, gain_hbm, bias_hbm, latent_hbm, weight_hbm, head_hbm,
    block_hbm, keys_hbm,
    raw_ref, gain_ref, bias_ref, latent_ref, weight_ref, head_ref,
    block_ref, keys_ref, sems,
):
    sources = (raw_hbm, gain_hbm, bias_hbm, latent_hbm, weight_hbm, head_hbm)
    targets = (raw_ref, gain_ref, bias_ref, latent_ref, weight_ref, head_ref)
    copies = [
        pltpu.make_async_copy(source, target, sems.at[i])
        for i, (source, target) in enumerate(zip(sources, targets))
    ]
    for copy in copies:
        copy.start()
    for copy in copies[:3]:
        copy.wait()
    values = raw_ref[...].astype(jnp.float32)
    center = jnp.mean(values, axis=-1, keepdims=True)
    moved = values - center
    spread = jnp.mean(jnp.square(moved), axis=-1, keepdims=True)
    scaled = moved * lax.rsqrt(spread + 1e-06)
    keys_ref[...] = (scaled * gain_ref[...] + bias_ref[...]).astype(jnp.bfloat16)
    outs = [pltpu.make_async_copy(keys_ref, keys_hbm, sems.at[0])]
    outs[-1].start()
    for copy in copies[3:]:
        copy.wait()
    block_ref[:TOKENS, :] = jnp.dot(
        latent_ref[...], weight_ref[...], preferred_element_type=jnp.float32
    ).astype(jnp.bfloat16)
    row = head_ref[...].astype(jnp.float32)
    tail_rows = ROWS - TOKENS
    row_at = lax.broadcasted_iota(jnp.int32, (tail_rows, HDIM), 0)
    first_row = jnp.broadcast_to(row[:, :HDIM], (tail_rows, HDIM))
    second_row = jnp.broadcast_to(row[:, HDIM:], (tail_rows, HDIM))
    block_ref[TOKENS:, :] = jnp.where(
        row_at == 0, first_row, jnp.where(row_at == 1, second_row, 0.0)
    ).astype(jnp.bfloat16)
    for i in range(block_hbm.shape[0]):
        outs.append(pltpu.make_async_copy(block_ref, block_hbm.at[i], sems.at[6 + i]))
        outs[-1].start()
    for copy in outs:
        copy.wait()


def front(arrays, copies):
    outs = (
        jax.ShapeDtypeStruct((copies, ROWS, HDIM), jnp.bfloat16),
        jax.ShapeDtypeStruct((KEYS, HDIM), jnp.bfloat16),
    )
    return pl.pallas_call(
        front_kernel,
        out_shape=outs,
        in_specs=[pl.BlockSpec(memory_space=HBM)] * len(arrays),
        out_specs=[pl.BlockSpec(memory_space=HBM)] * len(outs),
        scratch_shapes=[VMEM(a.shape, a.dtype) for a in arrays]
        + [VMEM(outs[0].shape[1:], jnp.bfloat16), VMEM(outs[1].shape, jnp.bfloat16)]
        + [pltpu.SemaphoreType.DMA((6 + copies,))],
        compiler_params=pltpu.CompilerParams(vmem_limit_bytes=60 * 2**20),
        cost_estimate=pl.CostEstimate(flops=2 * 256 * 1536 * 128, bytes_accessed=2 * 2**20, transcendentals=1024),
        name="front",
    )(*arrays)


def score_steps(part_refs, keys_refs, total_refs, flush, spans=None):
    spans = spans or [(0, p.shape[0]) for p in part_refs]
    heads = [(p, h) for p, span in zip(part_refs, spans) for h in range(*span)]
    blocks = TOKENS // TB
    steps = [(k, t, i) for k in range(len(keys_refs)) for t in range(blocks) for i in range(len(heads))]
    slots = AHEAD + 1

    def scoped(*accs):
        def acc(m, s, j):
            return accs[(m * slots + s) * 2 + j]

        zero = jnp.zeros((TB, HDIM), jnp.bfloat16)
        columns = [p[h, TOKENS:, :].astype(jnp.float32).T for p, h in heads]
        for k, keys_ref in enumerate(keys_refs):
            for m in range(2):
                a = keys_ref[512 * m : 512 * m + 256, :]
                b = keys_ref[512 * m + 256 : 512 * m + 512, :]
                pltpu.matmul_push_rhs(jnp.concatenate([a, b], axis=1), k, m, transpose=True)

        def issue(n):
            k, t, i = steps[n]
            p, h = heads[i]
            q = p[h, t * TB : (t + 1) * TB, :]
            low = jnp.concatenate([q, zero], axis=1)
            high = jnp.concatenate([zero, q], axis=1)
            staged = k if t == 0 and i == 0 else None
            for m in range(2):
                pltpu.matmul_acc_lhs(acc(m, n % slots, 0), low, load_staged_rhs=staged)
                pltpu.matmul_acc_lhs(acc(m, n % slots, 1), high)

        for n in range(AHEAD):
            issue(n)
        sums = None
        per_row = HDIM // TB
        for n, (k, t, i) in enumerate(steps):
            if n + AHEAD < len(steps):
                issue(n + AHEAD)
            rows = slice(t * TB, (t + 1) * TB)
            if i == 0:
                if not total_refs:
                    sums = [jnp.zeros((TB, 256), jnp.float32) for _ in range(4)]
                else:
                    sums = [total_refs[k][rows, 256 * g : 256 * (g + 1)] for g in range(4)]
            at = (t % per_row) * TB
            weight = columns[i][at : at + TB, t // per_row : t // per_row + 1]
            weight = jnp.broadcast_to(weight, (TB, 256))
            for m in range(2):
                for j in range(2):
                    score = pltpu.matmul_pop(acc(m, n % slots, j))
                    sums[2 * m + j] = sums[2 * m + j] + jnp.maximum(score, 0.0) * weight
            if i == len(heads) - 1:
                flush(k, t, sums)

    pl.run_scoped(scoped, *[pltpu.ACC(m)((TB, 256), jnp.float32) for m in range(2) for _ in range(2 * slots)])


def score_kernel(*refs, parts, sets, has_totals, has_place, spans):
    if has_place:
        place_ref, *refs, reach_ref = refs
        place = place_ref[...]
        key_begin = (place[:, 1:] * lax.axis_size("ha") + lax.axis_index("ha")) * KEYS
        reach_ref[...] = jnp.broadcast_to(place[:, :1] - key_begin, reach_ref.shape)
    part_refs, refs = refs[:parts], refs[parts:]
    keys_refs, refs = refs[:sets], refs[sets:]
    total_refs, out_refs = (refs[:sets], refs[sets:]) if has_totals else ((), refs)

    def flush(k, t, sums):
        rows = slice(t * TB, (t + 1) * TB)
        for g in range(4):
            out_refs[k][rows, 256 * g : 256 * (g + 1)] = sums[g].astype(out_refs[k].dtype)

    score_steps(part_refs, keys_refs, total_refs, flush, spans)


def score_cost(parts, sets):
    heads = sum(p.shape[0] for p in parts)
    return pl.CostEstimate(
        flops=heads * sets * 2**14, bytes_accessed=2**14, transcendentals=0
    )


def scores(parts, keys, totals=(), place=(), out_dtype=jnp.float32, spans=None, name="scores"):
    operands = (*place, *parts, *keys, *totals)
    outs = [jax.ShapeDtypeStruct((TOKENS, KEYS), out_dtype) for _ in keys]
    if place:
        outs.append(jax.ShapeDtypeStruct((TB, 256), jnp.int32))
    return pl.pallas_call(
        functools.partial(
            score_kernel,
            parts=len(parts),
            sets=len(keys),
            has_totals=bool(totals),
            has_place=bool(place),
            spans=spans,
        ),
        out_shape=outs,
        in_specs=[pl.BlockSpec(memory_space=VMEM)] * len(operands),
        out_specs=[pl.BlockSpec(memory_space=VMEM)] * len(outs),
        compiler_params=pltpu.CompilerParams(vmem_limit_bytes=24 * 2**20),
        cost_estimate=score_cost(parts, len(keys)),
        name=name,
    )(*operands)


def finish_kernel(part_ref, keys_ref, total_ref, reach_ref, other_ref, out_hbm, out_ref, sems):
    scale = HDIM ** (-0.5)
    reach = reach_ref[...]
    ahead = lax.broadcasted_iota(jnp.int32, (TB, 256), 1) - lax.broadcasted_iota(jnp.int32, (TB, 256), 0)
    copies = []

    def flush(k, t, sums):
        rows = slice(t * TB, (t + 1) * TB)
        for g in range(4):
            at = slice(256 * g, 256 * (g + 1))
            total = (sums[g] + other_ref[rows, at].astype(jnp.float32)) * scale
            out_ref[rows, at] = jnp.where(ahead <= reach + (t * TB - 256 * g), total, 0.0)
        copies.append(pltpu.make_async_copy(out_ref.at[rows], out_hbm.at[rows], sems.at[t]))
        copies[-1].start()
        if t == TOKENS // TB - 1:
            for copy in copies:
                copy.wait()

    score_steps((part_ref,), (keys_ref,), (total_ref,), flush, [(EARLY, part_ref.shape[0])])


def finish(part, keys, total, reach, other):
    return pl.pallas_call(
        finish_kernel,
        out_shape=jax.ShapeDtypeStruct((TOKENS, KEYS), jnp.float32),
        in_specs=[pl.BlockSpec(memory_space=VMEM)] * 5,
        out_specs=pl.BlockSpec(memory_space=HBM),
        scratch_shapes=[VMEM((TOKENS, KEYS), jnp.float32), pltpu.SemaphoreType.DMA((TOKENS // TB,))],
        compiler_params=pltpu.CompilerParams(vmem_limit_bytes=24 * 2**20),
        cost_estimate=score_cost((part,), 1),
        name="finish",
    )(part, keys, total, reach, other)


def layout(z_size, x_size):
    def flat(z, core, x):
        return ((z % z_size) * 2 + core) * x_size + x % x_size

    sites = [(z, x) for z in range(z_size) for x in range(x_size)]
    groups = [
        [flat(z, core, x) for z, x in sites if (z - x) % x_size == coset]
        for core in range(2)
        for coset in range(x_size)
    ]

    def moved(dz, dx):
        return [
            (flat(z, core, x), flat(z + sign * dz, core, x + sign * dx))
            for core, sign in ((0, 1), (1, -1))
            for z, x in sites
        ]

    swap = [(flat(z, core, x), flat(z, 1 - core, x)) for z, x in sites for core in range(2)]
    return groups, moved, swap


def per_device(
    latent, query_weight, head_weights, raw_keys, key_gain, key_bias, query_start, key_order
):
    ka, ha = lax.axis_size("ka"), lax.axis_size("ha")
    groups, moved, swap = layout(ka // 2, ha)
    gain, bias = key_gain.reshape(1, HDIM), key_bias.reshape(1, HDIM)
    head_row = head_weights.reshape(1, TOKENS)
    block, keys = front((raw_keys, gain, bias, latent, query_weight, head_row), len(groups[0]))
    here = lax.all_to_all(block, FLAT, 0, 0, axis_index_groups=groups)
    diagonal = lax.ppermute(here, FLAT, moved(1, -1))
    along_z = lax.ppermute(here, FLAT, moved(1, 0))
    along_x = lax.ppermute(here, FLAT, moved(0, 1))

    (own,) = scores((here,), (keys,), name="here_own")
    own, swapped = lax.optimization_barrier((own, keys))
    other_keys = lax.ppermute(swapped, FLAT, swap)
    place = (jnp.concatenate([query_start, key_order]).reshape(1, 2),)
    own, reach = scores((diagonal,), (keys,), (own,), place, name="diagonal_own")
    own, other_keys = lax.optimization_barrier((own, other_keys))
    (other,) = scores((here, diagonal), (other_keys,), name="here_diagonal_other")
    (other,) = scores((along_z,), (other_keys,), (other,), name="z_other")
    (other,) = scores((along_x,), (other_keys,), (other,), out_dtype=jnp.bfloat16, name="x_other")
    received = lax.ppermute(other, FLAT, swap)
    own, other = lax.optimization_barrier((own, other))
    spans = ((0, along_z.shape[0]), (0, EARLY))
    (own,) = scores((along_z, along_x), (keys,), (own,), spans=spans, name="z_own")
    return finish(along_x, keys, own, reach, received)


def solution(mesh):
    in_specs = (
        P("pb", None),
        P(None, ("ka", "ha")),
        P("pb", ("ka", "ha")),
        P(("ka", "ha"), None),
        P(),
        P(),
        P("pb"),
        P("ka"),
    )
    out_specs = P("pb", ("ka", "ha"))
    return jax.shard_map(
        per_device, mesh=mesh, in_specs=in_specs, out_specs=out_specs, check_vma=False
    )
```

```python
import functools

import jax
import jax.numpy as jnp
from jax import lax
from jax.experimental import pallas as pl
from jax.experimental.pallas import tpu as pltpu
from jax.sharding import PartitionSpec as P

VMEM = pltpu.VMEM
HBM = pltpu.HBM
TOKENS = 256
KEYS = 1024
HDIM = 128
ROWS = TOKENS + 16
TB = 32
AHEAD = 6
EARLY = 2
FLAT = ("ka", "ha")


def front_kernel(
    latent_hbm, weight_hbm, head_hbm, block_hbm, latent_ref, weight_ref, head_ref, block_ref, sems
):
    sources = (latent_hbm, weight_hbm, head_hbm)
    targets = (latent_ref, weight_ref, head_ref)
    copies = [
        pltpu.make_async_copy(source, target, sems.at[i])
        for i, (source, target) in enumerate(zip(sources, targets))
    ]
    for copy in copies:
        copy.start()
    for copy in copies:
        copy.wait()
    block_ref[:TOKENS, :] = jnp.dot(
        latent_ref[...], weight_ref[...], preferred_element_type=jnp.float32
    ).astype(jnp.bfloat16)
    row = head_ref[...].astype(jnp.float32)
    tail_rows = ROWS - TOKENS
    row_at = lax.broadcasted_iota(jnp.int32, (tail_rows, HDIM), 0)
    first = jnp.broadcast_to(row[:, :HDIM], (tail_rows, HDIM))
    second = jnp.broadcast_to(row[:, HDIM:], (tail_rows, HDIM))
    block_ref[TOKENS:, :] = jnp.where(
        row_at == 0, first, jnp.where(row_at == 1, second, 0.0)
    ).astype(jnp.bfloat16)
    outs = []
    for i in range(block_hbm.shape[0]):
        outs.append(pltpu.make_async_copy(block_ref, block_hbm.at[i], sems.at[i]))
        outs[-1].start()
    for copy in outs:
        copy.wait()


def front(arrays, copies):
    return pl.pallas_call(
        front_kernel,
        out_shape=jax.ShapeDtypeStruct((copies, ROWS, HDIM), jnp.bfloat16),
        in_specs=[pl.BlockSpec(memory_space=HBM)] * len(arrays),
        out_specs=pl.BlockSpec(memory_space=HBM),
        scratch_shapes=[VMEM(a.shape, a.dtype) for a in arrays]
        + [VMEM((ROWS, HDIM), jnp.bfloat16), pltpu.SemaphoreType.DMA((max(copies, len(arrays)),))],
        compiler_params=pltpu.CompilerParams(vmem_limit_bytes=60 * 2**20),
        cost_estimate=pl.CostEstimate(flops=2 * 256 * 1536 * 128, bytes_accessed=2 * 2**20, transcendentals=1024),
        name="front",
    )(*arrays)


def score_steps(part_refs, keys_refs, total_refs, flush, spans=None):
    spans = spans or [(0, p.shape[0]) for p in part_refs]
    heads = [(p, h) for p, span in zip(part_refs, spans) for h in range(*span)]
    blocks = TOKENS // TB
    steps = [(k, t, i) for k in range(len(keys_refs)) for t in range(blocks) for i in range(len(heads))]
    slots = AHEAD + 1

    def scoped(*accs):
        def acc(m, s, j):
            return accs[(m * slots + s) * 2 + j]

        zero = jnp.zeros((TB, HDIM), jnp.bfloat16)
        columns = [p[h, TOKENS:, :].astype(jnp.float32).T for p, h in heads]
        for k, keys_ref in enumerate(keys_refs):
            for m in range(2):
                a = keys_ref[512 * m : 512 * m + 256, :]
                b = keys_ref[512 * m + 256 : 512 * m + 512, :]
                pltpu.matmul_push_rhs(jnp.concatenate([a, b], axis=1), k, m, transpose=True)

        def issue(n):
            k, t, i = steps[n]
            p, h = heads[i]
            q = p[h, t * TB : (t + 1) * TB, :]
            low = jnp.concatenate([q, zero], axis=1)
            high = jnp.concatenate([zero, q], axis=1)
            staged = k if t == 0 and i == 0 else None
            for m in range(2):
                pltpu.matmul_acc_lhs(acc(m, n % slots, 0), low, load_staged_rhs=staged)
                pltpu.matmul_acc_lhs(acc(m, n % slots, 1), high)

        for n in range(AHEAD):
            issue(n)
        sums = None
        per_row = HDIM // TB
        for n, (k, t, i) in enumerate(steps):
            if n + AHEAD < len(steps):
                issue(n + AHEAD)
            rows = slice(t * TB, (t + 1) * TB)
            if i == 0:
                if not total_refs:
                    sums = [jnp.zeros((TB, 256), jnp.float32) for _ in range(4)]
                else:
                    sums = [total_refs[k][rows, 256 * g : 256 * (g + 1)] for g in range(4)]
            at = (t % per_row) * TB
            weight = columns[i][at : at + TB, t // per_row : t // per_row + 1]
            weight = jnp.broadcast_to(weight, (TB, 256))
            for m in range(2):
                for j in range(2):
                    score = pltpu.matmul_pop(acc(m, n % slots, j))
                    sums[2 * m + j] = sums[2 * m + j] + jnp.maximum(score, 0.0) * weight
            if i == len(heads) - 1:
                flush(k, t, sums)

    pl.run_scoped(scoped, *[pltpu.ACC(m)((TB, 256), jnp.float32) for m in range(2) for _ in range(2 * slots)])


def first_kernel(part_ref, raw_ref, gain_ref, bias_ref, total_ref, keys_ref):
    values = raw_ref[...].astype(jnp.float32)
    center = jnp.mean(values, axis=-1, keepdims=True)
    moved = values - center
    spread = jnp.mean(jnp.square(moved), axis=-1, keepdims=True)
    scaled = moved * lax.rsqrt(spread + 1e-06)
    keys_ref[...] = (scaled * gain_ref[...] + bias_ref[...]).astype(jnp.bfloat16)

    def flush(k, t, sums):
        for g in range(4):
            total_ref[t * TB : (t + 1) * TB, 256 * g : 256 * (g + 1)] = sums[g]

    score_steps((part_ref,), (keys_ref,), (), flush)


def first(part, raw_keys, gain, bias):
    return pl.pallas_call(
        first_kernel,
        out_shape=(
            jax.ShapeDtypeStruct((TOKENS, KEYS), jnp.float32),
            jax.ShapeDtypeStruct((KEYS, HDIM), jnp.bfloat16),
        ),
        in_specs=[pl.BlockSpec(memory_space=VMEM)] * 4,
        out_specs=[pl.BlockSpec(memory_space=VMEM)] * 2,
        compiler_params=pltpu.CompilerParams(vmem_limit_bytes=24 * 2**20),
        cost_estimate=score_cost((part,), 1),
        name="here_own",
    )(part, raw_keys, gain, bias)


def score_kernel(*refs, parts, sets, has_totals, has_place, spans):
    if has_place:
        start_ref, order_ref, *refs, reach_ref = refs
        key_begin = (order_ref[...] * lax.axis_size("ha") + lax.axis_index("ha")) * KEYS
        reach_ref[...] = jnp.broadcast_to(start_ref[...] - key_begin, reach_ref.shape)
    part_refs, refs = refs[:parts], refs[parts:]
    keys_refs, refs = refs[:sets], refs[sets:]
    total_refs, out_refs = (refs[:sets], refs[sets:]) if has_totals else ((), refs)

    def flush(k, t, sums):
        rows = slice(t * TB, (t + 1) * TB)
        for g in range(4):
            out_refs[k][rows, 256 * g : 256 * (g + 1)] = sums[g].astype(out_refs[k].dtype)

    score_steps(part_refs, keys_refs, total_refs, flush, spans)


def score_cost(parts, sets):
    heads = sum(p.shape[0] for p in parts)
    return pl.CostEstimate(
        flops=heads * sets * 2**14, bytes_accessed=2**14, transcendentals=0
    )


def scores(parts, keys, totals=(), place=(), out_dtype=jnp.float32, spans=None, name="scores"):
    operands = (*place, *parts, *keys, *totals)
    outs = [jax.ShapeDtypeStruct((TOKENS, KEYS), out_dtype) for _ in keys]
    if place:
        outs.append(jax.ShapeDtypeStruct((TB, 256), jnp.int32))
    return pl.pallas_call(
        functools.partial(
            score_kernel,
            parts=len(parts),
            sets=len(keys),
            has_totals=bool(totals),
            has_place=bool(place),
            spans=spans,
        ),
        out_shape=outs,
        in_specs=[pl.BlockSpec(memory_space=VMEM)] * len(operands),
        out_specs=[pl.BlockSpec(memory_space=VMEM)] * len(outs),
        compiler_params=pltpu.CompilerParams(vmem_limit_bytes=24 * 2**20),
        cost_estimate=score_cost(parts, len(keys)),
        name=name,
    )(*operands)


def finish_kernel(part_ref, keys_ref, total_ref, reach_ref, other_ref, out_hbm, out_ref, sems):
    scale = HDIM ** (-0.5)
    reach = reach_ref[...]
    ahead = lax.broadcasted_iota(jnp.int32, (TB, 256), 1) - lax.broadcasted_iota(jnp.int32, (TB, 256), 0)
    copies = []

    def flush(k, t, sums):
        rows = slice(t * TB, (t + 1) * TB)
        for g in range(4):
            at = slice(256 * g, 256 * (g + 1))
            total = (sums[g] + other_ref[rows, at].astype(jnp.float32)) * scale
            out_ref[rows, at] = jnp.where(ahead <= reach + (t * TB - 256 * g), total, 0.0)
        copies.append(pltpu.make_async_copy(out_ref.at[rows], out_hbm.at[rows], sems.at[t]))
        copies[-1].start()
        if t == TOKENS // TB - 1:
            for copy in copies:
                copy.wait()

    score_steps((part_ref,), (keys_ref,), (total_ref,), flush, [(EARLY, part_ref.shape[0])])


def finish(part, keys, total, reach, other):
    return pl.pallas_call(
        finish_kernel,
        out_shape=jax.ShapeDtypeStruct((TOKENS, KEYS), jnp.float32),
        in_specs=[pl.BlockSpec(memory_space=VMEM)] * 5,
        out_specs=pl.BlockSpec(memory_space=HBM),
        scratch_shapes=[VMEM((TOKENS, KEYS), jnp.float32), pltpu.SemaphoreType.DMA((TOKENS // TB,))],
        compiler_params=pltpu.CompilerParams(vmem_limit_bytes=24 * 2**20),
        cost_estimate=score_cost((part,), 1),
        name="finish",
    )(part, keys, total, reach, other)


def layout(z_size, x_size):
    def flat(z, core, x):
        return ((z % z_size) * 2 + core) * x_size + x % x_size

    sites = [(z, x) for z in range(z_size) for x in range(x_size)]
    groups = [
        [flat(z, core, x) for z, x in sites if (z - x) % x_size == coset]
        for core in range(2)
        for coset in range(x_size)
    ]

    def moved(dz, dx):
        return [
            (flat(z, core, x), flat(z + sign * dz, core, x + sign * dx))
            for core, sign in ((0, 1), (1, -1))
            for z, x in sites
        ]

    swap = [(flat(z, core, x), flat(z, 1 - core, x)) for z, x in sites for core in range(2)]
    return groups, moved, swap


def per_device(
    latent, query_weight, head_weights, raw_keys, key_gain, key_bias, query_start, key_order
):
    ka, ha = lax.axis_size("ka"), lax.axis_size("ha")
    groups, moved, swap = layout(ka // 2, ha)
    block = front((latent, query_weight, head_weights.reshape(1, TOKENS)), len(groups[0]))
    here = lax.all_to_all(block, FLAT, 0, 0, axis_index_groups=groups)
    diagonal = lax.ppermute(here, FLAT, moved(1, -1))
    along_z = lax.ppermute(here, FLAT, moved(1, 0))
    along_x = lax.ppermute(here, FLAT, moved(0, 1))

    own, keys = first(here, raw_keys, key_gain.reshape(1, HDIM), key_bias.reshape(1, HDIM))
    own, swapped = lax.optimization_barrier((own, keys))
    other_keys = lax.ppermute(swapped, FLAT, swap)
    place = (query_start.reshape(1, 1), key_order.reshape(1, 1))
    own, reach = scores((diagonal,), (keys,), (own,), place, name="diagonal_own")
    own, other_keys = lax.optimization_barrier((own, other_keys))
    (other,) = scores((here, diagonal), (other_keys,), name="here_diagonal_other")
    (other,) = scores((along_z,), (other_keys,), (other,), name="z_other")
    (other,) = scores((along_x,), (other_keys,), (other,), out_dtype=jnp.bfloat16, name="x_other")
    received = lax.ppermute(other, FLAT, swap)
    own, other = lax.optimization_barrier((own, other))
    spans = ((0, along_z.shape[0]), (0, EARLY))
    (own,) = scores((along_z, along_x), (keys,), (own,), spans=spans, name="z_own")
    return finish(along_x, keys, own, reach, received)


def solution(mesh):
    in_specs = (
        P("pb", None),
        P(None, ("ka", "ha")),
        P("pb", ("ka", "ha")),
        P(("ka", "ha"), None),
        P(),
        P(),
        P("pb"),
        P("ka"),
    )
    out_specs = P("pb", ("ka", "ha"))
    return jax.shard_map(
        per_device, mesh=mesh, in_specs=in_specs, out_specs=out_specs, check_vma=False
    )
```

```python
import functools

import jax
import jax.numpy as jnp
from jax import lax
from jax.experimental import pallas as pl
from jax.experimental.pallas import tpu as pltpu
from jax.sharding import PartitionSpec as P

VMEM = pltpu.VMEM
HBM = pltpu.HBM
TOKENS = 256
KEYS = 1024
HDIM = 128
ROWS = TOKENS + 16
TB = 32
AHEAD = 6
EARLY = 2
FLAT = ("ka", "ha")


def front_kernel(
    latent_hbm, weight_hbm, head_hbm, block_hbm, latent_ref, weight_ref, head_ref, block_ref, sems
):
    sources = (latent_hbm, weight_hbm, head_hbm)
    targets = (latent_ref, weight_ref, head_ref)
    copies = [
        pltpu.make_async_copy(source, target, sems.at[i])
        for i, (source, target) in enumerate(zip(sources, targets))
    ]
    for copy in copies:
        copy.start()
    for copy in copies:
        copy.wait()
    block_ref[:TOKENS, :] = jnp.dot(
        latent_ref[...], weight_ref[...], preferred_element_type=jnp.float32
    ).astype(jnp.bfloat16)
    row = head_ref[...].astype(jnp.float32)
    tail_rows = ROWS - TOKENS
    row_at = lax.broadcasted_iota(jnp.int32, (tail_rows, HDIM), 0)
    first = jnp.broadcast_to(row[:, :HDIM], (tail_rows, HDIM))
    second = jnp.broadcast_to(row[:, HDIM:], (tail_rows, HDIM))
    block_ref[TOKENS:, :] = jnp.where(
        row_at == 0, first, jnp.where(row_at == 1, second, 0.0)
    ).astype(jnp.bfloat16)
    outs = []
    for i in range(block_hbm.shape[0]):
        outs.append(pltpu.make_async_copy(block_ref, block_hbm.at[i], sems.at[i]))
        outs[-1].start()
    for copy in outs:
        copy.wait()


def front(arrays, copies):
    return pl.pallas_call(
        front_kernel,
        out_shape=jax.ShapeDtypeStruct((copies, ROWS, HDIM), jnp.bfloat16),
        in_specs=[pl.BlockSpec(memory_space=HBM)] * len(arrays),
        out_specs=pl.BlockSpec(memory_space=HBM),
        scratch_shapes=[VMEM(a.shape, a.dtype) for a in arrays]
        + [VMEM((ROWS, HDIM), jnp.bfloat16), pltpu.SemaphoreType.DMA((max(copies, len(arrays)),))],
        compiler_params=pltpu.CompilerParams(vmem_limit_bytes=60 * 2**20),
        cost_estimate=pl.CostEstimate(flops=2 * 256 * 1536 * 128, bytes_accessed=2 * 2**20, transcendentals=1024),
        name="front",
    )(*arrays)


def score_steps(part_refs, keys_refs, total_refs, flush, spans=None):
    spans = spans or [(0, p.shape[0]) for p in part_refs]
    heads = [(p, h) for p, span in zip(part_refs, spans) for h in range(*span)]
    blocks = TOKENS // TB
    steps = [(k, t, i) for k in range(len(keys_refs)) for t in range(blocks) for i in range(len(heads))]
    slots = AHEAD + 1

    def scoped(*accs):
        def acc(m, s, j):
            return accs[(m * slots + s) * 2 + j]

        zero = jnp.zeros((TB, HDIM), jnp.bfloat16)
        columns = [p[h, TOKENS:, :].astype(jnp.float32).T for p, h in heads]
        for k, keys_ref in enumerate(keys_refs):
            for m in range(2):
                a = keys_ref[512 * m : 512 * m + 256, :]
                b = keys_ref[512 * m + 256 : 512 * m + 512, :]
                pltpu.matmul_push_rhs(jnp.concatenate([a, b], axis=1), k, m, transpose=True)

        def issue(n):
            k, t, i = steps[n]
            p, h = heads[i]
            q = p[h, t * TB : (t + 1) * TB, :]
            low = jnp.concatenate([q, zero], axis=1)
            high = jnp.concatenate([zero, q], axis=1)
            staged = k if t == 0 and i == 0 else None
            for m in range(2):
                pltpu.matmul_acc_lhs(acc(m, n % slots, 0), low, load_staged_rhs=staged)
                pltpu.matmul_acc_lhs(acc(m, n % slots, 1), high)

        for n in range(AHEAD):
            issue(n)
        sums = None
        per_row = HDIM // TB
        for n, (k, t, i) in enumerate(steps):
            if n + AHEAD < len(steps):
                issue(n + AHEAD)
            rows = slice(t * TB, (t + 1) * TB)
            if i == 0:
                if not total_refs:
                    sums = [jnp.zeros((TB, 256), jnp.float32) for _ in range(4)]
                else:
                    sums = [total_refs[k][rows, 256 * g : 256 * (g + 1)] for g in range(4)]
            at = (t % per_row) * TB
            weight = columns[i][at : at + TB, t // per_row : t // per_row + 1]
            weight = jnp.broadcast_to(weight, (TB, 256))
            for m in range(2):
                for j in range(2):
                    score = pltpu.matmul_pop(acc(m, n % slots, j))
                    sums[2 * m + j] = sums[2 * m + j] + jnp.maximum(score, 0.0) * weight
            if i == len(heads) - 1:
                flush(k, t, sums)

    pl.run_scoped(scoped, *[pltpu.ACC(m)((TB, 256), jnp.float32) for m in range(2) for _ in range(2 * slots)])


def first_kernel(part_ref, raw_ref, gain_ref, bias_ref, total_ref, keys_ref):
    values = raw_ref[...].astype(jnp.float32)
    center = jnp.mean(values, axis=-1, keepdims=True)
    moved = values - center
    spread = jnp.mean(jnp.square(moved), axis=-1, keepdims=True)
    scaled = moved * lax.rsqrt(spread + 1e-06)
    keys_ref[...] = (scaled * gain_ref[...] + bias_ref[...]).astype(jnp.bfloat16)

    def flush(k, t, sums):
        for g in range(4):
            total_ref[t * TB : (t + 1) * TB, 256 * g : 256 * (g + 1)] = sums[g]

    score_steps((part_ref,), (keys_ref,), (), flush)


def first(part, raw_keys, gain, bias):
    return pl.pallas_call(
        first_kernel,
        out_shape=(
            jax.ShapeDtypeStruct((TOKENS, KEYS), jnp.float32),
            jax.ShapeDtypeStruct((KEYS, HDIM), jnp.bfloat16),
        ),
        in_specs=[pl.BlockSpec(memory_space=VMEM)] * 4,
        out_specs=[pl.BlockSpec(memory_space=VMEM)] * 2,
        compiler_params=pltpu.CompilerParams(vmem_limit_bytes=24 * 2**20),
        cost_estimate=score_cost((part,), 1),
        name="here_own",
    )(part, raw_keys, gain, bias)


def score_kernel(*refs, parts, sets, has_totals, has_place, spans):
    if has_place:
        start_ref, order_ref, *refs, reach_ref = refs
        key_begin = (order_ref[...] * lax.axis_size("ha") + lax.axis_index("ha")) * KEYS
        reach_ref[...] = jnp.broadcast_to(start_ref[...] - key_begin, reach_ref.shape)
    part_refs, refs = refs[:parts], refs[parts:]
    keys_refs, refs = refs[:sets], refs[sets:]
    total_refs, out_refs = (refs[:sets], refs[sets:]) if has_totals else ((), refs)

    def flush(k, t, sums):
        rows = slice(t * TB, (t + 1) * TB)
        for g in range(4):
            out_refs[k][rows, 256 * g : 256 * (g + 1)] = sums[g].astype(out_refs[k].dtype)

    score_steps(part_refs, keys_refs, total_refs, flush, spans)


def score_cost(parts, sets):
    heads = sum(p.shape[0] for p in parts)
    return pl.CostEstimate(
        flops=heads * sets * 2**14, bytes_accessed=2**14, transcendentals=0
    )


def scores(parts, keys, totals=(), place=(), out_dtype=jnp.float32, spans=None, name="scores"):
    operands = (*place, *parts, *keys, *totals)
    outs = [jax.ShapeDtypeStruct((TOKENS, KEYS), out_dtype) for _ in keys]
    if place:
        outs.append(jax.ShapeDtypeStruct((TB, 256), jnp.int32))
    return pl.pallas_call(
        functools.partial(
            score_kernel,
            parts=len(parts),
            sets=len(keys),
            has_totals=bool(totals),
            has_place=bool(place),
            spans=spans,
        ),
        out_shape=outs,
        in_specs=[pl.BlockSpec(memory_space=VMEM)] * len(operands),
        out_specs=[pl.BlockSpec(memory_space=VMEM)] * len(outs),
        compiler_params=pltpu.CompilerParams(vmem_limit_bytes=24 * 2**20),
        cost_estimate=score_cost(parts, len(keys)),
        name=name,
    )(*operands)


def finish_kernel(part_ref, keys_ref, total_ref, reach_ref, other_ref, out_hbm, out_ref, sems):
    scale = HDIM ** (-0.5)
    reach = reach_ref[...]
    ahead = lax.broadcasted_iota(jnp.int32, (TB, 256), 1) - lax.broadcasted_iota(jnp.int32, (TB, 256), 0)
    copies = []

    def flush(k, t, sums):
        rows = slice(t * TB, (t + 1) * TB)
        for g in range(4):
            at = slice(256 * g, 256 * (g + 1))
            total = (sums[g] + other_ref[rows, at].astype(jnp.float32)) * scale
            out_ref[rows, at] = jnp.where(ahead <= reach + (t * TB - 256 * g), total, 0.0)
        copies.append(pltpu.make_async_copy(out_ref.at[rows], out_hbm.at[rows], sems.at[t]))
        copies[-1].start()
        if t == TOKENS // TB - 1:
            for copy in copies:
                copy.wait()

    score_steps((part_ref,), (keys_ref,), (total_ref,), flush, [(EARLY, part_ref.shape[0])])


def finish(part, keys, total, reach, other):
    return pl.pallas_call(
        finish_kernel,
        out_shape=jax.ShapeDtypeStruct((TOKENS, KEYS), jnp.float32),
        in_specs=[pl.BlockSpec(memory_space=VMEM)] * 5,
        out_specs=pl.BlockSpec(memory_space=HBM),
        scratch_shapes=[VMEM((TOKENS, KEYS), jnp.float32), pltpu.SemaphoreType.DMA((TOKENS // TB,))],
        compiler_params=pltpu.CompilerParams(vmem_limit_bytes=24 * 2**20),
        cost_estimate=score_cost((part,), 1),
        name="finish",
    )(part, keys, total, reach, other)


def layout(z_size, x_size):
    def flat(z, core, x):
        return ((z % z_size) * 2 + core) * x_size + x % x_size

    sites = [(z, x) for z in range(z_size) for x in range(x_size)]
    groups = [
        [flat(z, core, x) for z, x in sites if (z - x) % x_size == coset]
        for core in range(2)
        for coset in range(x_size)
    ]

    def moved(dz, dx):
        return [
            (flat(z, core, x), flat(z + sign * dz, core, x + sign * dx))
            for core, sign in ((0, 1), (1, -1))
            for z, x in sites
        ]

    swap = [(flat(z, core, x), flat(z, 1 - core, x)) for z, x in sites for core in range(2)]
    return groups, moved, swap


def per_device(
    latent, query_weight, head_weights, raw_keys, key_gain, key_bias, query_start, key_order
):
    ka, ha = lax.axis_size("ka"), lax.axis_size("ha")
    groups, moved, swap = layout(ka // 2, ha)
    block = front((latent, query_weight, head_weights.reshape(1, TOKENS)), len(groups[0]))
    here = lax.all_to_all(block, FLAT, 0, 0, axis_index_groups=groups)
    diagonal = lax.ppermute(here, FLAT, moved(1, -1))
    along_z = lax.ppermute(here, FLAT, moved(1, 0))
    along_x = lax.ppermute(here, FLAT, moved(0, 1))

    own, keys = first(here, raw_keys, key_gain.reshape(1, HDIM), key_bias.reshape(1, HDIM))
    own, swapped = lax.optimization_barrier((own, keys))
    other_keys = lax.ppermute(swapped, FLAT, swap)
    (own,) = scores((diagonal,), (keys,), (own,), name="diagonal_own")
    own, other_keys = lax.optimization_barrier((own, other_keys))
    (other,) = scores((here, diagonal), (other_keys,), name="here_diagonal_other")
    other, own = scores((along_z,), (other_keys, keys), (other, own), name="z_both")
    (other,) = scores((along_x,), (other_keys,), (other,), out_dtype=jnp.bfloat16, name="x_other")
    received = lax.ppermute(other, FLAT, swap)
    own, other = lax.optimization_barrier((own, other))
    place = (query_start.reshape(1, 1), key_order.reshape(1, 1))
    own, reach = scores((along_x,), (keys,), (own,), place, spans=((0, EARLY),), name="x_early")
    return finish(along_x, keys, own, reach, received)


def solution(mesh):
    in_specs = (
        P("pb", None),
        P(None, ("ka", "ha")),
        P("pb", ("ka", "ha")),
        P(("ka", "ha"), None),
        P(),
        P(),
        P("pb"),
        P("ka"),
    )
    out_specs = P("pb", ("ka", "ha"))
    return jax.shard_map(
        per_device, mesh=mesh, in_specs=in_specs, out_specs=out_specs, check_vma=False
    )
```

```python
import functools

import jax
import jax.numpy as jnp
from jax import lax
from jax.experimental import pallas as pl
from jax.experimental.pallas import tpu as pltpu
from jax.sharding import PartitionSpec as P

VMEM = pltpu.VMEM
HBM = pltpu.HBM
TOKENS = 256
KEYS = 1024
HDIM = 128
ROWS = TOKENS + 16
TB = 32
AHEAD = 6
EARLY = 2
FLAT = ("ka", "ha")


def front_kernel(
    latent_hbm, weight_hbm, head_hbm, block_hbm, latent_ref, weight_ref, head_ref, block_ref, sems
):
    half = TOKENS // 2
    pairs = [(weight_hbm, weight_ref), (head_hbm, head_ref)]
    pairs += [(latent_hbm.at[pl.ds(i * half, half)], latent_ref.at[pl.ds(i * half, half)]) for i in range(2)]
    copies = [pltpu.make_async_copy(source, target, sems.at[i]) for i, (source, target) in enumerate(pairs)]
    for copy in copies:
        copy.start()
    for copy in copies[:2]:
        copy.wait()
    row = head_ref[...].astype(jnp.float32)
    tail_rows = ROWS - TOKENS
    row_at = lax.broadcasted_iota(jnp.int32, (tail_rows, HDIM), 0)
    first = jnp.broadcast_to(row[:, :HDIM], (tail_rows, HDIM))
    second = jnp.broadcast_to(row[:, HDIM:], (tail_rows, HDIM))
    block_ref[TOKENS:, :] = jnp.where(
        row_at == 0, first, jnp.where(row_at == 1, second, 0.0)
    ).astype(jnp.bfloat16)
    outs = []
    for i in range(2):
        copies[2 + i].wait()
        rows = slice(i * half, (i + 1) * half)
        block_ref[rows, :] = jnp.dot(
            latent_ref[rows, :], weight_ref[...], preferred_element_type=jnp.float32
        ).astype(jnp.bfloat16)
        part = pl.ds(i * half, half if i == 0 else ROWS - half)
        for n in range(block_hbm.shape[0]):
            sem = sems.at[4 + i * block_hbm.shape[0] + n]
            outs.append(pltpu.make_async_copy(block_ref.at[part], block_hbm.at[n, part], sem))
            outs[-1].start()
    for copy in outs:
        copy.wait()


def front(arrays, copies):
    return pl.pallas_call(
        front_kernel,
        out_shape=jax.ShapeDtypeStruct((copies, ROWS, HDIM), jnp.bfloat16),
        in_specs=[pl.BlockSpec(memory_space=HBM)] * len(arrays),
        out_specs=pl.BlockSpec(memory_space=HBM),
        scratch_shapes=[VMEM(a.shape, a.dtype) for a in arrays]
        + [VMEM((ROWS, HDIM), jnp.bfloat16), pltpu.SemaphoreType.DMA((4 + 2 * copies,))],
        compiler_params=pltpu.CompilerParams(vmem_limit_bytes=60 * 2**20),
        cost_estimate=pl.CostEstimate(flops=2 * 256 * 1536 * 128, bytes_accessed=2 * 2**20, transcendentals=1024),
        name="front",
    )(*arrays)


def score_steps(part_refs, keys_refs, total_refs, flush, spans=None):
    spans = spans or [(0, p.shape[0]) for p in part_refs]
    heads = [(p, h) for p, span in zip(part_refs, spans) for h in range(*span)]
    blocks = TOKENS // TB
    steps = [(k, t, i) for k in range(len(keys_refs)) for t in range(blocks) for i in range(len(heads))]
    slots = AHEAD + 1

    def scoped(*accs):
        def acc(m, s, j):
            return accs[(m * slots + s) * 2 + j]

        zero = jnp.zeros((TB, HDIM), jnp.bfloat16)
        columns = [p[h, TOKENS:, :].astype(jnp.float32).T for p, h in heads]
        for k, keys_ref in enumerate(keys_refs):
            for m in range(2):
                a = keys_ref[512 * m : 512 * m + 256, :]
                b = keys_ref[512 * m + 256 : 512 * m + 512, :]
                pltpu.matmul_push_rhs(jnp.concatenate([a, b], axis=1), k, m, transpose=True)

        def issue(n):
            k, t, i = steps[n]
            p, h = heads[i]
            q = p[h, t * TB : (t + 1) * TB, :]
            low = jnp.concatenate([q, zero], axis=1)
            high = jnp.concatenate([zero, q], axis=1)
            staged = k if t == 0 and i == 0 else None
            for m in range(2):
                pltpu.matmul_acc_lhs(acc(m, n % slots, 0), low, load_staged_rhs=staged)
                pltpu.matmul_acc_lhs(acc(m, n % slots, 1), high)

        for n in range(AHEAD):
            issue(n)
        sums = None
        per_row = HDIM // TB
        for n, (k, t, i) in enumerate(steps):
            if n + AHEAD < len(steps):
                issue(n + AHEAD)
            rows = slice(t * TB, (t + 1) * TB)
            if i == 0:
                if not total_refs:
                    sums = [jnp.zeros((TB, 256), jnp.float32) for _ in range(4)]
                else:
                    sums = [total_refs[k][rows, 256 * g : 256 * (g + 1)] for g in range(4)]
            at = (t % per_row) * TB
            weight = columns[i][at : at + TB, t // per_row : t // per_row + 1]
            weight = jnp.broadcast_to(weight, (TB, 256))
            for m in range(2):
                for j in range(2):
                    score = pltpu.matmul_pop(acc(m, n % slots, j))
                    sums[2 * m + j] = sums[2 * m + j] + jnp.maximum(score, 0.0) * weight
            if i == len(heads) - 1:
                flush(k, t, sums)

    pl.run_scoped(scoped, *[pltpu.ACC(m)((TB, 256), jnp.float32) for m in range(2) for _ in range(2 * slots)])


def first_kernel(part_ref, raw_ref, gain_ref, bias_ref, total_ref, keys_ref):
    values = raw_ref[...].astype(jnp.float32)
    center = jnp.mean(values, axis=-1, keepdims=True)
    moved = values - center
    spread = jnp.mean(jnp.square(moved), axis=-1, keepdims=True)
    scaled = moved * lax.rsqrt(spread + 1e-06)
    keys_ref[...] = (scaled * gain_ref[...] + bias_ref[...]).astype(jnp.bfloat16)

    def flush(k, t, sums):
        for g in range(4):
            total_ref[t * TB : (t + 1) * TB, 256 * g : 256 * (g + 1)] = sums[g]

    score_steps((part_ref,), (keys_ref,), (), flush)


def first(part, raw_keys, gain, bias):
    return pl.pallas_call(
        first_kernel,
        out_shape=(
            jax.ShapeDtypeStruct((TOKENS, KEYS), jnp.float32),
            jax.ShapeDtypeStruct((KEYS, HDIM), jnp.bfloat16),
        ),
        in_specs=[pl.BlockSpec(memory_space=VMEM)] * 4,
        out_specs=[pl.BlockSpec(memory_space=VMEM)] * 2,
        compiler_params=pltpu.CompilerParams(vmem_limit_bytes=24 * 2**20),
        cost_estimate=score_cost((part,), 1),
        name="here_own",
    )(part, raw_keys, gain, bias)


def score_kernel(*refs, parts, sets, has_totals, has_place, spans):
    if has_place:
        start_ref, order_ref, *refs, reach_ref = refs
        key_begin = (order_ref[...] * lax.axis_size("ha") + lax.axis_index("ha")) * KEYS
        reach_ref[...] = jnp.broadcast_to(start_ref[...] - key_begin, reach_ref.shape)
    part_refs, refs = refs[:parts], refs[parts:]
    keys_refs, refs = refs[:sets], refs[sets:]
    total_refs, out_refs = (refs[:sets], refs[sets:]) if has_totals else ((), refs)

    def flush(k, t, sums):
        rows = slice(t * TB, (t + 1) * TB)
        for g in range(4):
            out_refs[k][rows, 256 * g : 256 * (g + 1)] = sums[g].astype(out_refs[k].dtype)

    score_steps(part_refs, keys_refs, total_refs, flush, spans)


def score_cost(parts, sets):
    heads = sum(p.shape[0] for p in parts)
    return pl.CostEstimate(
        flops=heads * sets * 2**14, bytes_accessed=2**14, transcendentals=0
    )


def scores(parts, keys, totals=(), place=(), out_dtype=jnp.float32, spans=None, name="scores"):
    operands = (*place, *parts, *keys, *totals)
    outs = [jax.ShapeDtypeStruct((TOKENS, KEYS), out_dtype) for _ in keys]
    if place:
        outs.append(jax.ShapeDtypeStruct((TB, 256), jnp.int32))
    return pl.pallas_call(
        functools.partial(
            score_kernel,
            parts=len(parts),
            sets=len(keys),
            has_totals=bool(totals),
            has_place=bool(place),
            spans=spans,
        ),
        out_shape=outs,
        in_specs=[pl.BlockSpec(memory_space=VMEM)] * len(operands),
        out_specs=[pl.BlockSpec(memory_space=VMEM)] * len(outs),
        compiler_params=pltpu.CompilerParams(vmem_limit_bytes=24 * 2**20),
        cost_estimate=score_cost(parts, len(keys)),
        name=name,
    )(*operands)


def finish_kernel(part_ref, keys_ref, total_ref, reach_ref, other_ref, out_hbm, out_ref, sems):
    scale = HDIM ** (-0.5)
    reach = reach_ref[...]
    ahead = lax.broadcasted_iota(jnp.int32, (TB, 256), 1) - lax.broadcasted_iota(jnp.int32, (TB, 256), 0)
    copies = []

    def flush(k, t, sums):
        rows = slice(t * TB, (t + 1) * TB)
        for g in range(4):
            at = slice(256 * g, 256 * (g + 1))
            total = (sums[g] + other_ref[rows, at].astype(jnp.float32)) * scale
            out_ref[rows, at] = jnp.where(ahead <= reach + (t * TB - 256 * g), total, 0.0)
        copies.append(pltpu.make_async_copy(out_ref.at[rows], out_hbm.at[rows], sems.at[t]))
        copies[-1].start()
        if t == TOKENS // TB - 1:
            for copy in copies:
                copy.wait()

    score_steps((part_ref,), (keys_ref,), (total_ref,), flush, [(EARLY, part_ref.shape[0])])


def finish(part, keys, total, reach, other):
    return pl.pallas_call(
        finish_kernel,
        out_shape=jax.ShapeDtypeStruct((TOKENS, KEYS), jnp.float32),
        in_specs=[pl.BlockSpec(memory_space=VMEM)] * 5,
        out_specs=pl.BlockSpec(memory_space=HBM),
        scratch_shapes=[VMEM((TOKENS, KEYS), jnp.float32), pltpu.SemaphoreType.DMA((TOKENS // TB,))],
        compiler_params=pltpu.CompilerParams(vmem_limit_bytes=24 * 2**20),
        cost_estimate=score_cost((part,), 1),
        name="finish",
    )(part, keys, total, reach, other)


def layout(z_size, x_size):
    def flat(z, core, x):
        return ((z % z_size) * 2 + core) * x_size + x % x_size

    sites = [(z, x) for z in range(z_size) for x in range(x_size)]
    groups = [
        [flat(z, core, x) for z, x in sites if (z - x) % x_size == coset]
        for core in range(2)
        for coset in range(x_size)
    ]

    def moved(dz, dx):
        return [
            (flat(z, core, x), flat(z + sign * dz, core, x + sign * dx))
            for core, sign in ((0, 1), (1, -1))
            for z, x in sites
        ]

    swap = [(flat(z, core, x), flat(z, 1 - core, x)) for z, x in sites for core in range(2)]
    return groups, moved, swap


def per_device(
    latent, query_weight, head_weights, raw_keys, key_gain, key_bias, query_start, key_order
):
    ka, ha = lax.axis_size("ka"), lax.axis_size("ha")
    groups, moved, swap = layout(ka // 2, ha)
    block = front((latent, query_weight, head_weights.reshape(1, TOKENS)), len(groups[0]))
    here = lax.all_to_all(block, FLAT, 0, 0, axis_index_groups=groups)
    diagonal = lax.ppermute(here, FLAT, moved(1, -1))
    along_z = lax.ppermute(here, FLAT, moved(1, 0))
    along_x = lax.ppermute(here, FLAT, moved(0, 1))

    own, keys = first(here, raw_keys, key_gain.reshape(1, HDIM), key_bias.reshape(1, HDIM))
    own, swapped = lax.optimization_barrier((own, keys))
    other_keys = lax.ppermute(swapped, FLAT, swap)
    place = (query_start.reshape(1, 1), key_order.reshape(1, 1))
    own, reach = scores((diagonal,), (keys,), (own,), place, name="diagonal_own")
    own, other_keys = lax.optimization_barrier((own, other_keys))
    (other,) = scores((here, diagonal), (other_keys,), name="here_diagonal_other")
    (other,) = scores((along_z,), (other_keys,), (other,), name="z_other")
    (other,) = scores((along_x,), (other_keys,), (other,), out_dtype=jnp.bfloat16, name="x_other")
    received = lax.ppermute(other, FLAT, swap)
    own, other = lax.optimization_barrier((own, other))
    spans = ((0, along_z.shape[0]), (0, EARLY))
    (own,) = scores((along_z, along_x), (keys,), (own,), spans=spans, name="z_own")
    return finish(along_x, keys, own, reach, received)


def solution(mesh):
    in_specs = (
        P("pb", None),
        P(None, ("ka", "ha")),
        P("pb", ("ka", "ha")),
        P(("ka", "ha"), None),
        P(),
        P(),
        P("pb"),
        P("ka"),
    )
    out_specs = P("pb", ("ka", "ha"))
    return jax.shard_map(
        per_device, mesh=mesh, in_specs=in_specs, out_specs=out_specs, check_vma=False
    )
```
